128 devices in a mesh: dp: 32 (over x, y, core), mp: 4 (over z).
Axes of the slice: x: 4, y: 4, z: 4, core: 2. Of those that a mesh axis runs over, the one named last changes fastest.
Arguments:
- layer_input: bfloat16 [32, 1024, 2304], P('dp', 'mp'), may hold values from -6 to 6
- output_grad: bfloat16 [32, 1024, 9216], P('dp', None, 'mp'), may hold values from -0.046875 to 0.046875
- error_buffer: bfloat16 [32, 2304, 9216], P('dp', None, 'mp'), may hold values from -1.5 to 1.5
- q_start: float32 [9216, 32], P('mp'), may hold values from -6 to 6
Outputs:
- error_next: bfloat16 [32, 2304, 9216], P('dp', None, 'mp')
- p_basis: float32 [2304, 32], replicated
- q_next: float32 [9216, 32], P('mp')
The draws below stay inside these ranges and needn't reach their ends.
All inputs are finite; a program needn't handle non-finite values.
Results may differ from the reference program's by a relative error of at most 0.00045.
Values may be sent and summed in bfloat16 or wider, within the bound.
No kernel may reach another device: no remote copies, remote signals or barrier semaphores. Data moves between devices by JAX's collectives and lax.ppermute only.
A program may use at most 128 MiB of HBM per device.

```python
import jax
import jax.numpy as jnp
from jax import lax

ROWS = 2304
RANK = 32
TOK_DEV = 1024
COLS = 9216
REPLICAS = 32


def levels(own_key, shape, pieces, least, largest):
    level, own = 1.0, jax.random.fold_in(own_key, 6)
    for axis_at, parts in pieces:
        heights = jnp.exp(jax.random.uniform(jax.random.fold_in(own, axis_at), (parts,), jnp.float32, least / len(pieces), largest / len(pieces)))
        level = level * jnp.repeat(heights, shape[axis_at] // parts).reshape([-1 if axis == axis_at else 1 for axis in range(len(shape))])
    return level


def noise(rng, extent, width, reach, split=(), dtype=jnp.bfloat16):
    entries = jax.random.normal(rng, extent, jnp.float32) * width
    if len(split) > 0:
        entries = levels(rng, extent, split, -0.22, 0.18) * entries
    return jnp.clip(entries, min=-reach, max=reach).astype(dtype)


def setup_inputs(seed: int = 0) -> dict:
    keys = jax.random.split(jax.random.key(seed), 5)
    return {
        "layer_input": noise(keys[0], (REPLICAS, TOK_DEV, ROWS), 1.0, 6.0, ((0, 32), (1, 4))),
        "output_grad": noise(keys[1], (REPLICAS, TOK_DEV, COLS), (0.1 * TOK_DEV ** -0.5), 0.046875, ((0, 32), (2, 4))),
        "error_buffer": noise(keys[2], (REPLICAS, ROWS, COLS), 0.1, 1.5, ((0, 32), (2, 4))),
        "q_start": noise(keys[3], (COLS, RANK), 1.0, 6.0, ((0, 4),), jnp.float32),
    }


def make_combined(inputs, grads, errors):
    gradient = jnp.dot(inputs.T.astype(jnp.float32), grads.astype(jnp.float32), preferred_element_type=jnp.float32)
    return gradient + errors.astype(jnp.float32)

def reference(layer_input, output_grad, error_buffer, q_start):
    highest = lax.Precision.HIGHEST

    def left_term(carry, items):
        combined = make_combined(items[0], items[1], items[2])
        return (carry + jnp.dot(combined, q_start, precision=highest), None)
    p_sum, _ = lax.scan(left_term, jnp.zeros((ROWS, RANK), jnp.float32), (layer_input, output_grad, error_buffer))
    gram = jnp.dot(p_sum.T, p_sum, precision=highest)
    chol = jnp.linalg.cholesky(gram)
    p_basis = lax.linalg.triangular_solve(chol, p_sum, left_side=False, lower=True, transpose_a=True)

    def right_term(carry, items):
        combined = make_combined(items[0], items[1], items[2])
        return (carry + jnp.dot(combined.T, p_basis, precision=highest), None)
    q_sum, _ = lax.scan(right_term, jnp.zeros((COLS, RANK), jnp.float32), (layer_input, output_grad, error_buffer))
    q_next = q_sum / REPLICAS
    decompressed = jnp.dot(p_basis, q_next.T, precision=highest)

    def residual_of(items):
        combined = make_combined(items[0], items[1], items[2])
        return (combined - decompressed).astype(jnp.bfloat16)
    error_next = lax.map(residual_of, (layer_input, output_grad, error_buffer))
    return (error_next, p_basis, q_next)
```

```python
import jax
import jax.numpy as jnp
from jax import lax
from jax.experimental import pallas as pl
from jax.experimental.pallas import tpu as pltpu
from jax.sharding import Mesh, PartitionSpec as P

F32, BF16 = jnp.float32, jnp.bfloat16
MIB = 1 << 20
RANK = 32
NN = (((1,), (0,)), ((), ()))
NT = (((1,), (1,)), ((), ()))


def split3(x):
    hi = x.astype(BF16)
    rest = x - hi.astype(F32)
    mid = rest.astype(BF16)
    low = (rest - mid.astype(F32)).astype(BF16)
    return hi, mid, low


def stack3(x):
    return jnp.concatenate(split3(x), axis=0)


def fold3(x):
    return (x[2 * RANK:] + x[RANK:2 * RANK]) + x[:RANK]


def dot(a, b, dims):
    return lax.dot_general(a, b, dims, preferred_element_type=F32)


def params(limit, steps=1):
    return pltpu.CompilerParams(vmem_limit_bytes=limit * MIB, dimension_semantics=("arbitrary",) * steps)


def token_product_kernel(q_ref, g_ref, t_ref, q3_ref):
    @pl.when(pl.program_id(0) == 0)
    def _():
        q3_ref[...] = stack3(q_ref[...].T)

    t_ref[0] = fold3(dot(q3_ref[...], g_ref[...], NT))


def token_product(q, grads, parts):
    tokens, cols = grads.shape
    step = tokens // parts
    return pl.pallas_call(
        token_product_kernel,
        grid=(parts,),
        in_specs=[
            pl.BlockSpec((cols, RANK), lambda i: (0, 0)),
            pl.BlockSpec((step, cols), lambda i: (i, 0)),
        ],
        out_specs=[
            pl.BlockSpec((1, RANK, step), lambda i: (i, 0, 0)),
            pl.BlockSpec((3 * RANK, cols), lambda i: (0, 0)),
        ],
        out_shape=[
            jax.ShapeDtypeStruct((parts, RANK, step), F32),
            jax.ShapeDtypeStruct((3 * RANK, cols), BF16),
        ],
        compiler_params=params(32),
        name="token_product",
    )(q, grads)


def error_product_kernel(q3_ref, e_ref, p_ref):
    p_ref[...] = fold3(dot(q3_ref[...], e_ref[...], NT))


def error_product(q3, error):
    rows, cols = error.shape
    step = 256
    return pl.pallas_call(
        error_product_kernel,
        grid=(rows // step,),
        in_specs=[
            pl.BlockSpec((3 * RANK, cols), lambda i: (0, 0)),
            pl.BlockSpec((step, cols), lambda i: (i, 0)),
        ],
        out_specs=pl.BlockSpec((RANK, step), lambda i: (0, i)),
        out_shape=jax.ShapeDtypeStruct((RANK, rows), F32),
        compiler_params=params(32),
        name="error_product",
    )(q3, error)


def cut_halves(core, full_ref, keep_ref, send_ref):
    half = RANK // 2
    wide = full_ref.shape[1] // 128
    for ref, who in ((keep_ref, core), (send_ref, 1 - core)):
        rows = full_ref[pl.ds(pl.multiple_of(who * half, half), half), :]
        for r in range(half // 8):
            for k in range(wide):
                ref[r * wide + k] = rows[8 * r:8 * r + 8, 128 * k:128 * k + 128]


def join_halves(core, mine_ref, other_ref, full_ref):
    half = RANK // 2
    wide = full_ref.shape[1] // 128
    for ref, who in ((mine_ref, core), (other_ref, 1 - core)):
        for r in range(half // 8):
            rows = pl.ds(pl.multiple_of(who * half + 8 * r, 8), 8)
            for k in range(wide):
                full_ref[rows, 128 * k:128 * k + 128] = ref[r * wide + k]


def left_kernel(core_ref, t_ref, x_ref, e_ref, keep_ref, send_ref, full_ref):
    tokens = (t_ref[0] + t_ref[1]) + (t_ref[2] + t_ref[3])
    full_ref[...] = fold3(dot(stack3(tokens), x_ref[...], NN)) + e_ref[...]
    cut_halves(core_ref[0], full_ref, keep_ref, send_ref)


def left_partial(core, tokens, inputs, error_part):
    rows = inputs.shape[1]
    tiles = RANK // 16 * rows // 128
    half = jax.ShapeDtypeStruct((tiles, 8, 128), F32)
    vmem = pl.BlockSpec(memory_space=pltpu.VMEM)
    return pl.pallas_call(
        left_kernel,
        in_specs=[pl.BlockSpec(memory_space=pltpu.SMEM), vmem, vmem, vmem],
        out_specs=[vmem, vmem],
        out_shape=[half, half],
        scratch_shapes=[pltpu.VMEM((RANK, rows), F32)],
        compiler_params=pltpu.CompilerParams(vmem_limit_bytes=32 * MIB),
        name="left_partial",
    )(core, tokens, inputs, error_part)


def right_kernel(core_ref, mine_ref, other_ref, xt_ref, g_ref, e_ref, keep_ref, send_ref, p_ref, p3_ref, xp_ref, full_ref):
    i = pl.program_id(0)
    step = g_ref.shape[1]

    @pl.when(i == 0)
    def _():
        join_halves(core_ref[0], mine_ref, other_ref, p_ref)
        p3_ref[...] = stack3(p_ref[...])
        xp_ref[...] = stack3(fold3(dot(p3_ref[...], xt_ref[...], NN)))

    part = dot(p3_ref[...], e_ref[...], NN) + dot(xp_ref[...], g_ref[...], NN)
    full_ref[:, pl.ds(pl.multiple_of(i * step, step), step)] = fold3(part)

    @pl.when(i == pl.num_programs(0) - 1)
    def _():
        cut_halves(core_ref[0], full_ref, keep_ref, send_ref)


def right_partial(core, mine, other, inputs_t, grads, error):
    rows, cols = error.shape
    tokens = grads.shape[0]
    step = 256
    tiles = RANK // 16 * cols // 128
    half = jax.ShapeDtypeStruct((tiles, 8, 128), F32)
    whole = lambda *shape: pl.BlockSpec(shape, lambda i: (0,) * len(shape))
    return pl.pallas_call(
        right_kernel,
        grid=(cols // step,),
        in_specs=[
            pl.BlockSpec(memory_space=pltpu.SMEM),
            whole(*mine.shape),
            whole(*other.shape),
            whole(rows, tokens),
            pl.BlockSpec((tokens, step), lambda i: (0, i)),
            pl.BlockSpec((rows, step), lambda i: (0, i)),
        ],
        out_specs=[whole(tiles, 8, 128), whole(tiles, 8, 128), whole(RANK, rows)],
        out_shape=[half, half, jax.ShapeDtypeStruct((RANK, rows), F32)],
        scratch_shapes=[
            pltpu.VMEM((3 * RANK, rows), BF16),
            pltpu.VMEM((3 * RANK, tokens), BF16),
            pltpu.VMEM((RANK, cols), F32),
        ],
        compiler_params=params(40),
        name="right_partial",
    )(core, mine, other, inputs_t, grads, error)


def turn_kernel(at_ref, own_ref, left_ref, right_ref, far_left_ref, far_right_ref, out_ref):
    me = at_ref[0]
    step = own_ref.shape[0]
    half = step // 2

    def put(ref, owner, offset, size):
        at = pl.multiple_of(owner * step + offset, 128)
        out_ref[:, pl.ds(at, size)] = ref[...].T

    put(own_ref, me, 0, step)
    put(left_ref, lax.rem(me + 3, 4), 0, step)
    put(right_ref, lax.rem(me + 1, 4), 0, step)
    put(far_left_ref, lax.rem(me + 2, 4), 0, half)
    put(far_right_ref, lax.rem(me + 2, 4), half, half)


def turned_inputs(at, own, left, right, far_left, far_right):
    tokens, rows = own.shape
    step = 768
    block = lambda a: pl.BlockSpec((a.shape[0], step), lambda i: (0, i))
    arrays = (own, left, right, far_left, far_right)
    return pl.pallas_call(
        turn_kernel,
        grid=(rows // step,),
        in_specs=[pl.BlockSpec(memory_space=pltpu.SMEM)] + [block(a) for a in arrays],
        out_specs=pl.BlockSpec((step, 4 * tokens), lambda i: (i, 0)),
        out_shape=jax.ShapeDtypeStruct((rows, 4 * tokens), BF16),
        compiler_params=params(32),
        name="turned_inputs",
    )(at, *arrays)


def factor_kernel(p_ref, basis_ref, u6_ref, inv_ref):
    p = p_ref[...]
    gram = lax.dot_general(p, p, NT, precision=lax.Precision.HIGHEST, preferred_element_type=F32)
    row = lax.broadcasted_iota(jnp.int32, (RANK, 1), 0)
    eye = (row == lax.broadcasted_iota(jnp.int32, (RANK, RANK), 1)).astype(F32)
    both = jnp.concatenate([gram, eye], axis=1)
    scale = jnp.zeros((RANK, 1), F32)
    for k in range(RANK):
        pivot = both[k:k + 1, k:k + 1]
        scale = jnp.where(row == k, lax.rsqrt(pivot), scale)
        factor = jnp.where(row > k, both[:, k:k + 1] / pivot, 0.0)
        both = both - factor * both[k:k + 1, :]
    inverse = both[:, RANK:] * scale
    inv_ref[...] = inverse
    u = lax.dot_general(inverse, p, NN, precision=lax.Precision.HIGHEST, preferred_element_type=F32)
    u1, u2, u3 = (term.astype(F32) for term in split3(u))
    u6 = jnp.concatenate([u1, u2, u3, u1, u2, u1, u, jnp.zeros_like(u)], axis=0).T
    basis_ref[...] = u6[:, 6 * RANK:7 * RANK]
    u6_ref[...] = u6[:, :6 * RANK].astype(BF16)


def factor(p):
    rows = p.shape[1]
    vmem = pl.BlockSpec(memory_space=pltpu.VMEM)
    return pl.pallas_call(
        factor_kernel,
        in_specs=[vmem],
        out_specs=[vmem] * 3,
        out_shape=[
            jax.ShapeDtypeStruct((rows, RANK), F32),
            jax.ShapeDtypeStruct((rows, 6 * RANK), BF16),
            jax.ShapeDtypeStruct((RANK, RANK), F32),
        ],
        compiler_params=pltpu.CompilerParams(vmem_limit_bytes=32 * MIB),
        name="factor",
    )(p)


def residual_kernel(replicas, core_ref, mine_ref, other_ref, inv_ref, u_ref, xt_ref, g_ref, e_ref, out_ref, q_ref, w6_ref, full_ref):
    @pl.when(pl.program_id(0) == 0)
    def _():
        join_halves(core_ref[0], mine_ref, other_ref, full_ref)
        w = lax.dot_general(inv_ref[...], full_ref[...], NN, precision=lax.Precision.HIGHEST, preferred_element_type=F32)
        w = w * (1.0 / replicas)
        q_ref[...] = w.T
        w1, w2, w3 = split3(-w)
        w6_ref[...] = jnp.concatenate([w1, w1, w1, w2, w2, w3], axis=0)

    total = dot(xt_ref[...], g_ref[...], NN) + dot(u_ref[...], w6_ref[...], NN)
    out_ref[0] = (total + e_ref[...].astype(F32)).astype(BF16)


def residual(core, mine, other, inverse, u6, inputs_t, grads, error, replicas):
    rows, cols = error.shape
    tokens = grads.shape[0]
    step = 256
    whole = lambda *shape: pl.BlockSpec(shape, lambda i: (0,) * len(shape))
    import functools
    return pl.pallas_call(
        functools.partial(residual_kernel, replicas),
        grid=(rows // step,),
        in_specs=[
            pl.BlockSpec(memory_space=pltpu.SMEM),
            whole(*mine.shape),
            whole(*other.shape),
            whole(RANK, RANK),
            pl.BlockSpec((step, 6 * RANK), lambda i: (i, 0)),
            pl.BlockSpec((step, tokens), lambda i: (i, 0)),
            whole(tokens, cols),
            pl.BlockSpec((step, cols), lambda i: (i, 0)),
        ],
        out_specs=[pl.BlockSpec((1, step, cols), lambda i: (0, i, 0)), whole(cols, RANK)],
        out_shape=[jax.ShapeDtypeStruct((1, rows, cols), BF16), jax.ShapeDtypeStruct((cols, RANK), F32)],
        scratch_shapes=[pltpu.VMEM((6 * RANK, cols), BF16), pltpu.VMEM((RANK, cols), F32)],
        compiler_params=params(56),
        name="residual",
    )(core, mine, other, inverse, u6, inputs_t, grads, error)


def swap(x, axis, pairs):
    return lax.ppermute(x, axis, [(a, b) for a, b in pairs] + [(b, a) for a, b in pairs])


def shift(x, by):
    return lax.ppermute(x, "z", [(i, (i + by) % 4) for i in range(4)])


def total(keep, send, over_z):
    tiles = keep.shape[0]
    places = 16
    each = -(-tiles // places)
    half = keep + swap(send, "c", [(0, 1)])
    half = jnp.pad(half, ((0, places * each - tiles), (0, 0), (0, 0)))
    parts = lax.all_to_all(half.reshape(places, each, 8, 128), ("x", "y"), 0, 0)
    part = jnp.sum(parts, axis=0)
    if over_z:
        part = part + swap(part, "z", [(0, 1), (2, 3)])
        part = part + swap(part, "z", [(1, 2), (3, 0)])
    spread = jnp.broadcast_to(part, (places,) + part.shape)
    mine = lax.all_to_all(spread, ("x", "y"), 0, 0).reshape(places * each, 8, 128)[:tiles]
    return mine, swap(mine, "c", [(0, 1)])


def local(layer_input, output_grad, error_buffer, q_start):
    inputs, grads, error = layer_input[0], output_grad[0], error_buffer[0]
    core = lax.axis_index("c").astype(jnp.int32)[None]
    at = lax.axis_index("z").astype(jnp.int32)[None]
    replicas = 32

    tokens, q3 = token_product(q_start, grads, 4)
    tokens = lax.all_to_all(tokens, "z", 0, 0)
    left = shift(inputs, 1)
    right = shift(inputs, -1)
    error_part = error_product(q3, error)
    keep, send = left_partial(core, tokens, inputs, error_part)
    half = inputs.shape[0] // 2
    far_left = shift(left[:half], 1)
    far_right = shift(right[half:], -1)
    mine, other = total(keep, send, True)
    inputs_t = turned_inputs(at, inputs, left, right, far_left, far_right)
    keep, send, p = right_partial(core, mine, other, inputs_t, grads, error)
    basis, u6, inverse = factor(p)
    mine, other = total(keep, send, False)
    error_next, q_next = residual(core, mine, other, inverse, u6, inputs_t, grads, error, replicas)
    return error_next, basis, q_next


def solution(mesh):
    fine = Mesh(mesh.devices.reshape(4, 4, 2, 4), ("x", "y", "c", "z"))
    dp = ("x", "y", "c")
    in_specs = (P(dp, "z", None), P(dp, None, "z"), P(dp, None, "z"), P("z", None))
    out_specs = (P(dp, None, "z"), P(), P("z", None))
    return jax.shard_map(local, mesh=fine, in_specs=in_specs, out_specs=out_specs, check_vma=False)
```

```python
import functools

import jax
import jax.numpy as jnp
from jax import lax
from jax.experimental import pallas as pl
from jax.experimental.pallas import tpu as pltpu
from jax.sharding import Mesh, PartitionSpec as P

F32, BF16 = jnp.float32, jnp.bfloat16
MIB = 1 << 20
RANK = 32
NN = (((1,), (0,)), ((), ()))
NT = (((1,), (1,)), ((), ()))


def split3(x):
    hi = x.astype(BF16)
    rest = x - hi.astype(F32)
    mid = rest.astype(BF16)
    low = (rest - mid.astype(F32)).astype(BF16)
    return hi, mid, low


def stack3(x):
    return jnp.concatenate(split3(x), axis=0)


def fold3(x):
    return (x[2 * RANK:] + x[RANK:2 * RANK]) + x[:RANK]


def dot(a, b, dims):
    return lax.dot_general(a, b, dims, preferred_element_type=F32)


VMEM_SPEC = pl.BlockSpec(memory_space=pltpu.VMEM)
HBM_SPEC = pl.BlockSpec(memory_space=pltpu.HBM)
SMEM_SPEC = pl.BlockSpec(memory_space=pltpu.SMEM)


def here(x):
    return pltpu.with_memory_space_constraint(x, pltpu.VMEM)


def there(x):
    return pltpu.with_memory_space_constraint(x, pltpu.HBM)


def call(kernel, name, arrays, in_specs, out_shape, out_specs, limit, scratch=(), flops=0, moved=0):
    return pl.pallas_call(
        kernel,
        in_specs=in_specs,
        out_specs=out_specs,
        out_shape=out_shape,
        scratch_shapes=list(scratch),
        compiler_params=pltpu.CompilerParams(vmem_limit_bytes=limit * MIB),
        cost_estimate=pl.CostEstimate(flops=int(flops), bytes_accessed=int(moved), transcendentals=0),
        name=name,
    )(*arrays)


def row_copy(source, target, sems, step, i):
    rows = pl.ds(pl.multiple_of(i * step, step), step)
    return pltpu.make_async_copy(source.at[rows], target.at[rows], sems.at[i])


def start_rows(source, target, sems, step):
    for i in range(source.shape[0] // step):
        row_copy(source, target, sems, step, i).start()


def for_rows(source, target, sems, step, work):
    def body(i, carry):
        row_copy(source, target, sems, step, i).wait()
        work(i)
        return carry

    lax.fori_loop(0, source.shape[0] // step, body, 0)


def turned_fold(x):
    return fold3(x.T[:3 * RANK])


def three_terms(q_t):
    terms = [term.astype(F32) for term in split3(q_t)]
    return jnp.concatenate(terms + [jnp.zeros_like(terms[0])], axis=0).T.astype(BF16)


def token_product_kernel(q_hbm, g_hbm, x_hbm, t_ref, top_ref, bottom_ref, q_ref, q3_ref, g_ref, sems, g_sems):
    step = 512
    part = t_ref.shape[2]
    half = top_ref.shape[0]
    q_copy = pltpu.make_async_copy(q_hbm, q_ref, sems.at[0])
    halves = [
        pltpu.make_async_copy(x_hbm.at[pl.ds(0, half)], top_ref, sems.at[1]),
        pltpu.make_async_copy(x_hbm.at[pl.ds(half, half)], bottom_ref, sems.at[2]),
    ]
    q_copy.start()
    start_rows(g_hbm, g_ref, g_sems, step)
    for copy in halves:
        copy.start()
    q_copy.wait()
    q3_ref[...] = three_terms(q_ref[...])

    def work(i):
        for k in range(step // part):
            rows = pl.ds(pl.multiple_of(i * step + k * part, part), part)
            t_ref[i * (step // part) + k] = turned_fold(dot(g_ref[rows, :], q3_ref[...], NN))

    for_rows(g_hbm, g_ref, g_sems, step, work)
    for copy in halves:
        copy.wait()


def token_product(q_t, grads, inputs, parts):
    tokens, cols = grads.shape
    half = inputs.shape[0] // 2
    return call(
        token_product_kernel, "token_product", (there(q_t), there(grads), there(inputs)), [HBM_SPEC] * 3,
        [
            pltpu.VMEM((parts, RANK, tokens // parts), F32),
            pltpu.VMEM((half, inputs.shape[1]), BF16),
            pltpu.VMEM((half, inputs.shape[1]), BF16),
        ],
        [VMEM_SPEC] * 3, 16,
        [
            pltpu.VMEM(q_t.shape, F32),
            pltpu.VMEM((cols, 4 * RANK), BF16),
            pltpu.VMEM((tokens, cols), BF16),
            pltpu.SemaphoreType.DMA((3,)),
            pltpu.SemaphoreType.DMA((tokens // 512,)),
        ],
        2 * 256 * tokens * cols, 2 * tokens * cols,
    )


def error_product_kernel(q_hbm, e_hbm, p_ref, q_ref, q3_ref, e_ref, sem, sems):
    step = 768
    q_copy = pltpu.make_async_copy(q_hbm, q_ref, sem)
    q_copy.start()
    start_rows(e_hbm, e_ref, sems, step)
    q_copy.wait()
    q3_ref[...] = three_terms(q_ref[...])

    def work(i):
        rows = pl.ds(pl.multiple_of(i * step, step), step)
        p_ref[:, rows] = turned_fold(dot(e_ref[rows, :], q3_ref[...], NN))

    for_rows(e_hbm, e_ref, sems, step, work)


def error_product(q_t, error):
    rows, cols = error.shape
    return call(
        error_product_kernel, "error_product", (there(q_t), there(error)), [HBM_SPEC] * 2,
        pltpu.VMEM((RANK, rows), F32), VMEM_SPEC, 16,
        [
            pltpu.VMEM(q_t.shape, F32),
            pltpu.VMEM((cols, 4 * RANK), BF16),
            pltpu.VMEM((rows, cols), BF16),
            pltpu.SemaphoreType.DMA,
            pltpu.SemaphoreType.DMA((rows // 768,)),
        ],
        10e9, 0,
    )


def cut_halves(core, full_ref, keep_ref, send_ref):
    half = RANK // 2
    wide = full_ref.shape[1] // 128
    for ref, who in ((keep_ref, core), (send_ref, 1 - core)):
        rows = full_ref[pl.ds(pl.multiple_of(who * half, half), half), :]
        for r in range(half // 8):
            for k in range(wide):
                ref[r * wide + k] = rows[8 * r:8 * r + 8, 128 * k:128 * k + 128]


def join_halves(core, mine_ref, other_ref, full_ref):
    half = RANK // 2
    wide = full_ref.shape[1] // 128
    for ref, who in ((mine_ref, core), (other_ref, 1 - core)):
        for r in range(half // 8):
            rows = pl.ds(pl.multiple_of(who * half + 8 * r, 8), 8)
            for k in range(wide):
                full_ref[rows, 128 * k:128 * k + 128] = ref[r * wide + k]


def left_kernel(core_ref, t_ref, x_ref, e_ref, keep_ref, send_ref, full_ref):
    tokens = (t_ref[0] + t_ref[1]) + (t_ref[2] + t_ref[3])
    full_ref[...] = fold3(dot(stack3(tokens), x_ref[...], NN)) + e_ref[...]
    cut_halves(core_ref[0], full_ref, keep_ref, send_ref)


def left_partial(core, tokens, inputs, error_part):
    rows = inputs.shape[1]
    half = pltpu.VMEM((RANK // 16 * rows // 128, 8, 128), F32)
    return call(
        left_kernel, "left_partial", (core, tokens, inputs, here(error_part)), [SMEM_SPEC] + [VMEM_SPEC] * 3,
        [half, half], [VMEM_SPEC] * 2, 12, [pltpu.VMEM((RANK, rows), F32)],
        2 * 256 * inputs.size, 2 * inputs.size,
    )


def right_kernel(core_ref, mine_ref, other_ref, xt_ref, g_ref, e_ref, keep_ref, send_ref, p_ref, p3_ref, xp_ref, full_ref):
    join_halves(core_ref[0], mine_ref, other_ref, p_ref)
    p3_ref[...] = stack3(p_ref[...])
    xp_ref[...] = stack3(fold3(dot(p3_ref[...], xt_ref[...], NN)))
    step = 256
    for i in range(g_ref.shape[1] // step):
        cols = slice(i * step, (i + 1) * step)
        full_ref[:, cols] = fold3(dot(p3_ref[...], e_ref[:, cols], NN) + dot(xp_ref[...], g_ref[:, cols], NN))
    cut_halves(core_ref[0], full_ref, keep_ref, send_ref)


def right_partial(core, mine, other, inputs_t, grads, error):
    rows, cols = error.shape
    tokens = grads.shape[0]
    half = pltpu.VMEM((RANK // 16 * cols // 128, 8, 128), F32)
    return call(
        right_kernel, "right_partial", (core, mine, other, here(inputs_t), here(grads), here(error)),
        [SMEM_SPEC] + [VMEM_SPEC] * 5,
        [half, half, pltpu.VMEM((RANK, rows), F32)], [VMEM_SPEC] * 3, 12,
        [
            pltpu.VMEM((3 * RANK, rows), BF16),
            pltpu.VMEM((3 * RANK, tokens), BF16),
            pltpu.VMEM((RANK, cols), F32),
        ],
        2 * 256 * (rows * cols + tokens * (rows + cols)), 0,
    )


def turn_kernel(places, at_ref, *refs):
    out_ref = refs[-1]
    tokens = out_ref.shape[1] // 4
    for (by, half), ref in zip(places, refs):
        owner = lax.rem(at_ref[0] + by, 4)
        start = pl.multiple_of(owner * tokens + half * (tokens // 2), 128)
        out_ref[:, pl.ds(start, ref.shape[0])] = ref[...].T


def turned(places, at, pieces, earlier=None, flops=0):
    rows = pieces[0].shape[1]
    arrays = tuple(pieces) if earlier is None else (*pieces, here(earlier))
    return pl.pallas_call(
        functools.partial(turn_kernel, places),
        in_specs=[SMEM_SPEC] + [VMEM_SPEC] * len(arrays),
        out_specs=VMEM_SPEC,
        out_shape=pltpu.VMEM((rows, 8 * pieces[-1].shape[0]), BF16),
        input_output_aliases={} if earlier is None else {len(arrays): 0},
        compiler_params=pltpu.CompilerParams(vmem_limit_bytes=12 * MIB),
        cost_estimate=pl.CostEstimate(flops=int(flops), bytes_accessed=0, transcendentals=0),
        name="turned",
    )(at, *arrays)


def load_kernel(g_hbm, e_hbm, g_ref, e_ref, sems):
    copies = [pltpu.make_async_copy(g_hbm, g_ref, sems.at[0]), pltpu.make_async_copy(e_hbm, e_ref, sems.at[1])]
    for copy in copies:
        copy.start()
    for copy in copies:
        copy.wait()


def loaded(grads, error):
    return call(
        load_kernel, "loaded", (there(grads), there(error)), [HBM_SPEC] * 2,
        [pltpu.VMEM(grads.shape, BF16), pltpu.VMEM(error.shape, BF16)], [VMEM_SPEC] * 2, 12,
        [pltpu.SemaphoreType.DMA((2,))], 0, 2 * (grads.size + error.size),
    )


def combined_kernel(at, rows, xt_ref, g_ref, e_ref, c_ref):
    here_rows = slice(at * rows, (at + 1) * rows)
    step = 256
    for i in range(g_ref.shape[1] // step):
        cols = slice(i * step, (i + 1) * step)
        c_ref[:, cols] = dot(xt_ref[here_rows, :], g_ref[:, cols], NN) + e_ref[here_rows, cols].astype(F32)


def combined(at, parts, inputs_t, grads, error):
    rows, cols = error.shape
    rows //= parts
    return call(
        functools.partial(combined_kernel, at, rows), "combined", (here(inputs_t), here(grads), here(error)),
        [VMEM_SPEC] * 3, pltpu.VMEM((rows, cols), F32), VMEM_SPEC, 12, (),
        2 * rows * cols * grads.shape[0], 0,
    )


def factor_kernel(p_ref, basis_ref, u6_ref, inv_ref):
    p = p_ref[...]
    gram = lax.dot_general(p, p, NT, precision=lax.Precision.HIGHEST, preferred_element_type=F32)
    row = lax.broadcasted_iota(jnp.int32, (RANK, 1), 0)
    eye = (row == lax.broadcasted_iota(jnp.int32, (RANK, RANK), 1)).astype(F32)
    both = jnp.concatenate([gram, eye], axis=1)
    scale = jnp.zeros((RANK, 1), F32)
    for k in range(RANK):
        pivot = both[k:k + 1, k:k + 1]
        scale = jnp.where(row == k, lax.rsqrt(pivot), scale)
        factor = jnp.where(row > k, both[:, k:k + 1] / pivot, 0.0)
        both = both - factor * both[k:k + 1, :]
    inverse = both[:, RANK:] * scale
    inv_ref[...] = inverse
    u = lax.dot_general(inverse, p, NN, precision=lax.Precision.HIGHEST, preferred_element_type=F32)
    u1, u2, u3 = (term.astype(F32) for term in split3(u))
    u6 = jnp.concatenate([u1, u2, u3, u1, u2, u1, u, jnp.zeros_like(u)], axis=0).T
    basis_ref[...] = u
    u6_ref[...] = u6[:, :6 * RANK].astype(BF16)


def factor(p):
    rows = p.shape[1]
    return call(
        factor_kernel, "factor", (here(p),), [VMEM_SPEC],
        [pltpu.VMEM((RANK, rows), F32), pltpu.VMEM((rows, 6 * RANK), BF16), pltpu.VMEM((RANK, RANK), F32)],
        [VMEM_SPEC] * 3, 12, (), 4e9, 0,
    )


def residual_kernel(replicas, core_ref, mine_ref, other_ref, inv_ref, u_ref, *refs):
    *c_refs, out_hbm, q_ref, full_ref, w6_ref, block_ref, sems = refs
    join_halves(core_ref[0], mine_ref, other_ref, full_ref)
    w = lax.dot_general(inv_ref[...], full_ref[...], NN, precision=lax.Precision.HIGHEST, preferred_element_type=F32)
    w = w * (1.0 / replicas)
    q_ref[...] = w
    w1, w2, w3 = split3(-w)
    w6_ref[...] = jnp.concatenate([w1, w1, w1, w2, w2, w3], axis=0)
    slots, step, width = block_ref.shape
    each = c_refs[0].shape[0] // step

    def copy_out(i):
        rows = pl.ds(pl.multiple_of(i * step, step), step)
        slot = lax.rem(i, slots)
        return pltpu.make_async_copy(block_ref.at[slot], out_hbm.at[0, rows], sems.at[slot])

    def part(s, c_ref):
        def body(k, carry):
            i = s * each + k
            slot = lax.rem(i, slots)
            rows = pl.ds(pl.multiple_of(i * step, step), step)
            c_rows = pl.ds(pl.multiple_of(k * step, step), step)

            @pl.when(i >= slots)
            def _():
                copy_out(i - slots).wait()

            for at in range(0, width, 256):
                cols = slice(at, at + 256)
                update = dot(u_ref[rows, :], w6_ref[:, cols], NN)
                block_ref[slot, :, cols] = (c_ref[c_rows, cols] + update).astype(BF16)
            copy_out(i).start()
            return carry

        lax.fori_loop(0, each, body, 0)

    for s, c_ref in enumerate(c_refs):
        part(s, c_ref)
    count = each * len(c_refs)
    for i in range(count - slots, count):
        copy_out(i).wait()


def residual(core, mine, other, inverse, u6, parts, replicas):
    cols = parts[0].shape[1]
    rows = len(parts) * parts[0].shape[0]
    step = parts[0].shape[0] // 2
    return call(
        functools.partial(residual_kernel, replicas), "residual",
        (core, mine, other, here(inverse), here(u6), *(here(part) for part in parts)),
        [SMEM_SPEC] + [VMEM_SPEC] * (4 + len(parts)),
        [pltpu.HBM((1, rows, cols), BF16), jax.ShapeDtypeStruct((RANK, cols), F32)],
        [HBM_SPEC, VMEM_SPEC], 12,
        [
            pltpu.VMEM((RANK, cols), F32),
            pltpu.VMEM((6 * RANK, cols), BF16),
            pltpu.VMEM((3, step, cols), BF16),
            pltpu.SemaphoreType.DMA((3,)),
        ],
        2 * 256 * rows * cols, 2 * rows * cols,
    )


def swap(x, axis, pairs):
    return lax.ppermute(x, axis, [(a, b) for a, b in pairs] + [(b, a) for a, b in pairs])


def shift(x, by):
    return lax.ppermute(x, "z", [(i, (i + by) % 4) for i in range(4)])


FIRST, SECOND = [(0, 1), (2, 3)], [(1, 2), (3, 0)]


def after(reason, *arrays):
    return lax.optimization_barrier((reason, *arrays))[1:]


def add_swapped(x, axis, pairs, *with_it):
    moved = swap(x, axis, pairs)
    return x + lax.optimization_barrier((moved, *with_it))[0]


def local(layer_input, output_grad, error_buffer, q_start):
    inputs, grads, error = layer_input[0], output_grad[0], error_buffer[0]
    core = lax.axis_index("c").astype(jnp.int32)[None]
    at = lax.axis_index("z").astype(jnp.int32)[None]
    replicas = 32
    tokens, top, bottom = token_product(q_start.T, grads, inputs, 4)
    (q_t,) = after(tokens, q_start.T)
    tokens = lax.all_to_all(tokens, "z", 0, 0)
    left_a, right_b = shift(top, 1), shift(bottom, -1)
    error_part = error_product(q_t, error)
    keep, send = left_partial(core, tokens, inputs, error_part)
    p = keep + swap(send, "c", [(0, 1)])
    bottom, top = after(p, bottom, top)
    left_b, right_a = shift(bottom, 1), shift(top, -1)
    p = add_swapped(p, "x", FIRST)
    inputs_t = turned(((0, 0), (3, 0), (1, 1)), at, after(p, inputs, left_a, right_b))
    p = add_swapped(p, "x", SECOND, inputs_t)
    far_a, far_b = after(p, left_a, right_b)
    far_a, far_b = shift(far_a, 1), shift(far_b, -1)
    p = add_swapped(p, "y", FIRST)
    grads, error = loaded(*after(p, grads, error))
    p = add_swapped(p, "y", SECOND, grads, error)
    left_b, right_a, inputs_t = after(p, left_b, right_a, inputs_t)
    inputs_t = turned(((3, 1), (1, 0)), at, (left_b, right_a), inputs_t, 4e9)
    p = add_swapped(p, "z", FIRST, inputs_t)
    far_a, far_b, inputs_t = after(p, far_a, far_b, inputs_t)
    inputs_t = turned(((2, 0), (2, 1)), at, (far_a, far_b), inputs_t)
    part = lambda s, reason: combined(s, 4, *after(reason, inputs_t, grads, error))
    parts = [part(0, p)]
    p = add_swapped(p, "z", SECOND, parts[0])
    keep, send, p = right_partial(core, p, swap(p, "c", [(0, 1)]), inputs_t, grads, error)

    q = keep + swap(send, "c", [(0, 1)])
    for s, (axis, pairs) in enumerate((("x", FIRST), ("x", SECOND), ("y", FIRST))):
        parts.append(part(s + 1, q))
        q = add_swapped(q, axis, pairs, parts[-1])
    basis, u6, inverse = factor(*after(q, p))
    q = add_swapped(q, "y", SECOND, basis)
    other = swap(q, "c", [(0, 1)])
    error_next, q_next = residual(core, q, other, inverse, u6, parts, replicas)
    return error_next, basis.T, q_next.T


def solution(mesh):
    fine = Mesh(mesh.devices.reshape(4, 4, 2, 4), ("x", "y", "c", "z"))
    dp = ("x", "y", "c")
    in_specs = (P(dp, "z", None), P(dp, None, "z"), P(dp, None, "z"), P("z", None))
    out_specs = (P(dp, None, "z"), P(), P("z", None))
    return jax.shard_map(local, mesh=fine, in_specs=in_specs, out_specs=out_specs, check_vma=False)
```

```python
import functools

import jax
import jax.numpy as jnp
from jax import lax
from jax.experimental import pallas as pl
from jax.experimental.pallas import tpu as pltpu
from jax.sharding import Mesh, PartitionSpec as P

F32, BF16 = jnp.float32, jnp.bfloat16
MIB = 1 << 20
RANK = 32
NN = (((1,), (0,)), ((), ()))
NT = (((1,), (1,)), ((), ()))


def split3(x):
    hi = x.astype(BF16)
    rest = x - hi.astype(F32)
    mid = rest.astype(BF16)
    low = (rest - mid.astype(F32)).astype(BF16)
    return hi, mid, low


def stack3(x):
    return jnp.concatenate(split3(x), axis=0)


def fold3(x):
    return (x[2 * RANK:] + x[RANK:2 * RANK]) + x[:RANK]


def dot(a, b, dims):
    return lax.dot_general(a, b, dims, preferred_element_type=F32)


VMEM_SPEC = pl.BlockSpec(memory_space=pltpu.VMEM)
HBM_SPEC = pl.BlockSpec(memory_space=pltpu.HBM)
SMEM_SPEC = pl.BlockSpec(memory_space=pltpu.SMEM)


def here(x):
    return pltpu.with_memory_space_constraint(x, pltpu.VMEM)


def there(x):
    return pltpu.with_memory_space_constraint(x, pltpu.HBM)


def call(kernel, name, arrays, in_specs, out_shape, out_specs, limit, scratch=(), flops=0, moved=0):
    return pl.pallas_call(
        kernel,
        in_specs=in_specs,
        out_specs=out_specs,
        out_shape=out_shape,
        scratch_shapes=list(scratch),
        compiler_params=pltpu.CompilerParams(vmem_limit_bytes=limit * MIB),
        cost_estimate=pl.CostEstimate(flops=int(flops), bytes_accessed=int(moved), transcendentals=0),
        name=name,
    )(*arrays)


def row_copy(source, target, sems, step, i):
    rows = pl.ds(pl.multiple_of(i * step, step), step)
    return pltpu.make_async_copy(source.at[rows], target.at[rows], sems.at[i])


def start_rows(source, target, sems, step):
    for i in range(source.shape[0] // step):
        row_copy(source, target, sems, step, i).start()


def for_rows(source, target, sems, step, work):
    def body(i, carry):
        row_copy(source, target, sems, step, i).wait()
        work(i)
        return carry

    lax.fori_loop(0, source.shape[0] // step, body, 0)


def turned_fold(x):
    return fold3(x.T[:3 * RANK])


def three_terms(q_t):
    terms = [term.astype(F32) for term in split3(q_t)]
    return jnp.concatenate(terms + [jnp.zeros_like(terms[0])], axis=0).T.astype(BF16)


def token_product_kernel(core_ref, q_hbm, g_hbm, x_hbm, t_ref, top_ref, bottom_ref, q_ref, q3_ref, g_ref, sems, g_sems):
    step = 512
    part = t_ref.shape[2]
    half = top_ref.shape[0]
    q_copy = pltpu.make_async_copy(q_hbm, q_ref, sems.at[0])
    halves = [
        pltpu.make_async_copy(x_hbm.at[pl.ds(0, half)], top_ref, sems.at[1]),
        pltpu.make_async_copy(x_hbm.at[pl.ds(half, half)], bottom_ref, sems.at[2]),
    ]
    q_copy.start()
    start_rows(g_hbm, g_ref, g_sems, step)
    for copy in halves:
        copy.start()

    @pl.when(core_ref[0] >= 0)
    def _():
        q_copy.wait()
        q3_ref[...] = three_terms(q_ref[...])

    def work(i):
        for k in range(step // part):
            rows = pl.ds(pl.multiple_of(i * step + k * part, part), part)
            t_ref[i * (step // part) + k] = turned_fold(dot(g_ref[rows, :], q3_ref[...], NN))

    for_rows(g_hbm, g_ref, g_sems, step, work)
    for copy in halves:
        copy.wait()


def token_product(core, q_t, grads, inputs, parts):
    tokens, cols = grads.shape
    half = inputs.shape[0] // 2
    return call(
        token_product_kernel, "token_product", (core, there(q_t), there(grads), there(inputs)), [SMEM_SPEC] + [HBM_SPEC] * 3,
        [
            pltpu.VMEM((parts, RANK, tokens // parts), F32),
            pltpu.VMEM((half, inputs.shape[1]), BF16),
            pltpu.VMEM((half, inputs.shape[1]), BF16),
        ],
        [VMEM_SPEC] * 3, 16,
        [
            pltpu.VMEM(q_t.shape, F32),
            pltpu.VMEM((cols, 4 * RANK), BF16),
            pltpu.VMEM((tokens, cols), BF16),
            pltpu.SemaphoreType.DMA((3,)),
            pltpu.SemaphoreType.DMA((tokens // 512,)),
        ],
        2 * 256 * tokens * cols, 2 * tokens * cols,
    )


def error_product_kernel(core_ref, q_hbm, e_hbm, p_ref, q_ref, q3_ref, e_ref, sem, sems):
    step = 768
    q_copy = pltpu.make_async_copy(q_hbm, q_ref, sem)
    q_copy.start()
    start_rows(e_hbm, e_ref, sems, step)

    @pl.when(core_ref[0] >= 0)
    def _():
        q_copy.wait()
        q3_ref[...] = three_terms(q_ref[...])

    def work(i):
        rows = pl.ds(pl.multiple_of(i * step, step), step)
        p_ref[:, rows] = turned_fold(dot(e_ref[rows, :], q3_ref[...], NN))

    for_rows(e_hbm, e_ref, sems, step, work)


def error_product(core, q_t, error):
    rows, cols = error.shape
    return call(
        error_product_kernel, "error_product", (core, there(q_t), there(error)), [SMEM_SPEC] + [HBM_SPEC] * 2,
        pltpu.VMEM((RANK, rows), F32), VMEM_SPEC, 16,
        [
            pltpu.VMEM(q_t.shape, F32),
            pltpu.VMEM((cols, 4 * RANK), BF16),
            pltpu.VMEM((rows, cols), BF16),
            pltpu.SemaphoreType.DMA,
            pltpu.SemaphoreType.DMA((rows // 768,)),
        ],
        10e9, 0,
    )


def cut_halves(core, full_ref, keep_ref, send_ref):
    half = RANK // 2
    wide = full_ref.shape[1] // 128
    for ref, who in ((keep_ref, core), (send_ref, 1 - core)):
        rows = full_ref[pl.ds(pl.multiple_of(who * half, half), half), :]
        for r in range(half // 8):
            for k in range(wide):
                ref[r * wide + k] = rows[8 * r:8 * r + 8, 128 * k:128 * k + 128]


def join_halves(core, mine_ref, other_ref, full_ref):
    half = RANK // 2
    wide = full_ref.shape[1] // 128
    for ref, who in ((mine_ref, core), (other_ref, 1 - core)):
        for r in range(half // 8):
            rows = pl.ds(pl.multiple_of(who * half + 8 * r, 8), 8)
            for k in range(wide):
                full_ref[rows, 128 * k:128 * k + 128] = ref[r * wide + k]


def left_kernel(core_ref, t_ref, x_ref, e_ref, keep_ref, send_ref, full_ref):
    tokens = (t_ref[0] + t_ref[1]) + (t_ref[2] + t_ref[3])
    full_ref[...] = fold3(dot(stack3(tokens), x_ref[...], NN)) + e_ref[...]
    cut_halves(core_ref[0], full_ref, keep_ref, send_ref)


def left_partial(core, tokens, inputs, error_part):
    rows = inputs.shape[1]
    half = pltpu.VMEM((RANK // 16 * rows // 128, 8, 128), F32)
    return call(
        left_kernel, "left_partial", (core, tokens, inputs, here(error_part)), [SMEM_SPEC] + [VMEM_SPEC] * 3,
        [half, half], [VMEM_SPEC] * 2, 12, [pltpu.VMEM((RANK, rows), F32)],
        2 * 256 * inputs.size, 2 * inputs.size,
    )


def right_kernel(core_ref, mine_ref, other_ref, xt_ref, g_ref, e_ref, keep_ref, send_ref, p_ref, p3_ref, xp_ref, full_ref):
    join_halves(core_ref[0], mine_ref, other_ref, p_ref)
    p3_ref[...] = stack3(p_ref[...])
    xp_ref[...] = stack3(fold3(dot(p3_ref[...], xt_ref[...], NN)))
    step = 256
    for i in range(g_ref.shape[1] // step):
        cols = slice(i * step, (i + 1) * step)
        full_ref[:, cols] = fold3(dot(p3_ref[...], e_ref[:, cols], NN) + dot(xp_ref[...], g_ref[:, cols], NN))
    cut_halves(core_ref[0], full_ref, keep_ref, send_ref)


def right_partial(core, mine, other, inputs_t, grads, error):
    rows, cols = error.shape
    tokens = grads.shape[0]
    half = pltpu.VMEM((RANK // 16 * cols // 128, 8, 128), F32)
    return call(
        right_kernel, "right_partial", (core, mine, other, here(inputs_t), here(grads), here(error)),
        [SMEM_SPEC] + [VMEM_SPEC] * 5,
        [half, half, pltpu.VMEM((RANK, rows), F32)], [VMEM_SPEC] * 3, 12,
        [
            pltpu.VMEM((3 * RANK, rows), BF16),
            pltpu.VMEM((3 * RANK, tokens), BF16),
            pltpu.VMEM((RANK, cols), F32),
        ],
        2 * 256 * (rows * cols + tokens * (rows + cols)), 0,
    )


def turn_kernel(places, at_ref, *refs):
    out_ref = refs[-1]
    tokens = out_ref.shape[1] // 4
    for (by, half), ref in zip(places, refs):
        owner = lax.rem(at_ref[0] + by, 4)
        start = pl.multiple_of(owner * tokens + half * (tokens // 2), 128)
        out_ref[:, pl.ds(start, ref.shape[0])] = ref[...].T


def turned(places, at, pieces, earlier=None, flops=0):
    rows = pieces[0].shape[1]
    arrays = tuple(pieces) if earlier is None else (*pieces, here(earlier))
    return pl.pallas_call(
        functools.partial(turn_kernel, places),
        in_specs=[SMEM_SPEC] + [VMEM_SPEC] * len(arrays),
        out_specs=VMEM_SPEC,
        out_shape=pltpu.VMEM((rows, 8 * pieces[-1].shape[0]), BF16),
        input_output_aliases={} if earlier is None else {len(arrays): 0},
        compiler_params=pltpu.CompilerParams(vmem_limit_bytes=12 * MIB),
        cost_estimate=pl.CostEstimate(flops=int(flops), bytes_accessed=0, transcendentals=0),
        name="turned",
    )(at, *arrays)


def load_kernel(source, target, sem):
    copy = pltpu.make_async_copy(source, target, sem)
    copy.start()
    copy.wait()


def loaded(x, cost):
    return call(
        load_kernel, "loaded", (there(x),), [HBM_SPEC], pltpu.VMEM(x.shape, x.dtype), VMEM_SPEC, 12,
        [pltpu.SemaphoreType.DMA], cost, 0,
    )


def combined_kernel(at, rows, xt_ref, g_ref, e_ref, c_ref):
    here_rows = slice(at * rows, (at + 1) * rows)
    step = 256
    for i in range(g_ref.shape[1] // step):
        cols = slice(i * step, (i + 1) * step)
        c_ref[:, cols] = dot(xt_ref[here_rows, :], g_ref[:, cols], NN) + e_ref[here_rows, cols].astype(F32)


def combined(at, parts, inputs_t, grads, error):
    rows, cols = error.shape
    rows //= parts
    return call(
        functools.partial(combined_kernel, at, rows), "combined", (here(inputs_t), here(grads), here(error)),
        [VMEM_SPEC] * 3, pltpu.VMEM((rows, cols), F32), VMEM_SPEC, 12, (),
        2 * rows * cols * grads.shape[0], 0,
    )


def factor_kernel(p_ref, basis_ref, u6_ref, inv_ref):
    p = p_ref[...]
    gram = lax.dot_general(p, p, NT, precision=lax.Precision.HIGHEST, preferred_element_type=F32)
    row = lax.broadcasted_iota(jnp.int32, (RANK, 1), 0)
    eye = (row == lax.broadcasted_iota(jnp.int32, (RANK, RANK), 1)).astype(F32)
    both = jnp.concatenate([gram, eye], axis=1)
    scale = jnp.zeros((RANK, 1), F32)
    for k in range(RANK):
        pivot = both[k:k + 1, k:k + 1]
        scale = jnp.where(row == k, lax.rsqrt(pivot), scale)
        factor = jnp.where(row > k, both[:, k:k + 1] / pivot, 0.0)
        both = both - factor * both[k:k + 1, :]
    inverse = both[:, RANK:] * scale
    i1, i2, i3 = (term.astype(F32) for term in split3(inverse))
    inv_ref[...] = jnp.concatenate([i1, i1, i1, i2, i2, i3], axis=1).astype(BF16)
    u = lax.dot_general(inverse, p, NN, precision=lax.Precision.HIGHEST, preferred_element_type=F32)
    u1, u2, u3 = (term.astype(F32) for term in split3(u))
    u6 = jnp.concatenate([u1, u2, u3, u1, u2, u1, u, jnp.zeros_like(u)], axis=0).T
    basis_ref[...] = u
    u6_ref[...] = u6[:, :6 * RANK].astype(BF16)


def factor(p):
    rows = p.shape[1]
    return call(
        factor_kernel, "factor", (here(p),), [VMEM_SPEC],
        [pltpu.VMEM((RANK, rows), F32), pltpu.VMEM((rows, 6 * RANK), BF16), pltpu.VMEM((RANK, 6 * RANK), BF16)],
        [VMEM_SPEC] * 3, 12, (), 4e9, 0,
    )


def residual_kernel(replicas, core_ref, mine_ref, other_ref, inv_ref, u_ref, *refs):
    *c_refs, out_hbm, q_ref, full_ref, w6_ref, block_ref, sems = refs
    join_halves(core_ref[0], mine_ref, other_ref, full_ref)
    q1, q2, q3 = split3(full_ref[...])
    w = dot(inv_ref[...], jnp.concatenate([q1, q2, q3, q1, q2, q1], axis=0), NN) * (1.0 / replicas)
    q_ref[...] = w
    w1, w2, w3 = split3(-w)
    w6_ref[...] = jnp.concatenate([w1, w1, w1, w2, w2, w3], axis=0)
    slots, step, width = block_ref.shape
    each = c_refs[0].shape[0] // step

    def copy_out(i):
        rows = pl.ds(pl.multiple_of(i * step, step), step)
        slot = lax.rem(i, slots)
        return pltpu.make_async_copy(block_ref.at[slot], out_hbm.at[0, rows], sems.at[slot])

    def part(s, c_ref):
        def body(k, carry):
            i = s * each + k
            slot = lax.rem(i, slots)
            rows = pl.ds(pl.multiple_of(i * step, step), step)
            c_rows = pl.ds(pl.multiple_of(k * step, step), step)

            @pl.when(i >= slots)
            def _():
                copy_out(i - slots).wait()

            for at in range(0, width, 256):
                cols = slice(at, at + 256)
                update = dot(u_ref[rows, :], w6_ref[:, cols], NN)
                block_ref[slot, :, cols] = (c_ref[c_rows, cols] + update).astype(BF16)
            copy_out(i).start()
            return carry

        lax.fori_loop(0, each, body, 0)

    for s, c_ref in enumerate(c_refs):
        part(s, c_ref)
    count = each * len(c_refs)
    for i in range(count - slots, count):
        copy_out(i).wait()


def residual(core, mine, other, inverse, u6, parts, replicas):
    cols = parts[0].shape[1]
    rows = len(parts) * parts[0].shape[0]
    step = parts[0].shape[0] // 2
    return call(
        functools.partial(residual_kernel, replicas), "residual",
        (core, mine, other, here(inverse), here(u6), *(here(part) for part in parts)),
        [SMEM_SPEC] + [VMEM_SPEC] * (4 + len(parts)),
        [pltpu.HBM((1, rows, cols), BF16), jax.ShapeDtypeStruct((RANK, cols), F32)],
        [HBM_SPEC, VMEM_SPEC], 12,
        [
            pltpu.VMEM((RANK, cols), F32),
            pltpu.VMEM((6 * RANK, cols), BF16),
            pltpu.VMEM((3, step, cols), BF16),
            pltpu.SemaphoreType.DMA((3,)),
        ],
        2 * 256 * rows * cols, 2 * rows * cols,
    )


def swap(x, axis, pairs):
    return lax.ppermute(x, axis, [(a, b) for a, b in pairs] + [(b, a) for a, b in pairs])


def shift(x, by):
    return lax.ppermute(x, "z", [(i, (i + by) % 4) for i in range(4)])


FIRST, SECOND = [(0, 1), (2, 3)], [(1, 2), (3, 0)]


def after(reason, *arrays):
    return lax.optimization_barrier((reason, *arrays))[1:]


def add_swapped(x, axis, pairs, *with_it):
    moved = swap(x, axis, pairs)
    return x + lax.optimization_barrier((moved, *with_it))[0]


def local(layer_input, output_grad, error_buffer, q_start):
    inputs, grads, error = layer_input[0], output_grad[0], error_buffer[0]
    core = lax.axis_index("c").astype(jnp.int32)[None]
    at = lax.axis_index("z").astype(jnp.int32)[None]
    replicas = 32
    tokens, top, bottom = token_product(core, q_start.T, grads, inputs, 4)
    (q_t,) = after(tokens, q_start.T)
    tokens = lax.all_to_all(tokens, "z", 0, 0)
    left_a, right_b = shift(top, 1), shift(bottom, -1)
    error_part = error_product(core, q_t, error)
    keep, send = left_partial(core, tokens, inputs, error_part)
    p = keep + swap(send, "c", [(0, 1)])
    p = add_swapped(p, "z", FIRST)
    bottom, top = after(p, bottom, top)
    left_b, right_a = shift(bottom, 1), shift(top, -1)
    inputs_t = turned(((0, 0), (3, 0), (1, 1)), at, after(p, inputs, left_a, right_b), None, 4e9)
    p = add_swapped(p, "z", SECOND, inputs_t)
    far_a, far_b = after(p, left_a, right_b)
    far_a, far_b = shift(far_a, 1), shift(far_b, -1)
    p = add_swapped(p, "x", FIRST)
    error = loaded(*after(p, error), 4e9)
    p = add_swapped(p, "x", SECOND, error)
    left_b, right_a, inputs_t, grads = after(p, left_b, right_a, inputs_t, grads)
    grads = loaded(grads, 2e9)
    inputs_t = turned(((3, 1), (1, 0)), at, (left_b, right_a), inputs_t, 2e9)
    p = add_swapped(p, "y", FIRST, grads, inputs_t)
    far_a, far_b, inputs_t = after(p, far_a, far_b, inputs_t)
    inputs_t = turned(((2, 0), (2, 1)), at, (far_a, far_b), inputs_t, 0)
    p = add_swapped(p, "y", SECOND, inputs_t)
    keep, send, p = right_partial(core, p, swap(p, "c", [(0, 1)]), inputs_t, grads, error)

    q = keep + swap(send, "c", [(0, 1)])
    basis, u6, inverse = factor(*after(q, p))
    q = add_swapped(q, "x", FIRST, basis)
    parts = []
    for s, (axis, pairs) in enumerate((("x", SECOND), ("y", FIRST), ("y", SECOND))):
        parts.append(combined(s, 3, *after(q, inputs_t, grads, error)))
        q = add_swapped(q, axis, pairs, parts[-1])
    other = swap(q, "c", [(0, 1)])
    error_next, q_next = residual(core, q, other, inverse, u6, parts, replicas)
    return error_next, basis.T, q_next.T


def solution(mesh):
    fine = Mesh(mesh.devices.reshape(4, 4, 2, 4), ("x", "y", "c", "z"))
    dp = ("x", "y", "c")
    in_specs = (P(dp, "z", None), P(dp, None, "z"), P(dp, None, "z"), P("z", None))
    out_specs = (P(dp, None, "z"), P(), P("z", None))
    return jax.shard_map(local, mesh=fine, in_specs=in_specs, out_specs=out_specs, check_vma=False)
```

```python
import functools

import jax
import jax.numpy as jnp
from jax import lax
from jax.experimental import pallas as pl
from jax.experimental.pallas import tpu as pltpu
from jax.sharding import Mesh, PartitionSpec as P

F32, BF16 = jnp.float32, jnp.bfloat16
MIB = 1 << 20
RANK = 32
NN = (((1,), (0,)), ((), ()))
NT = (((1,), (1,)), ((), ()))


def split3(x):
    hi = x.astype(BF16)
    rest = x - hi.astype(F32)
    mid = rest.astype(BF16)
    low = (rest - mid.astype(F32)).astype(BF16)
    return hi, mid, low


def stack3(x):
    return jnp.concatenate(split3(x), axis=0)


def fold3(x):
    return (x[2 * RANK:] + x[RANK:2 * RANK]) + x[:RANK]


def dot(a, b, dims):
    return lax.dot_general(a, b, dims, preferred_element_type=F32)


VMEM_SPEC = pl.BlockSpec(memory_space=pltpu.VMEM)
HBM_SPEC = pl.BlockSpec(memory_space=pltpu.HBM)
SMEM_SPEC = pl.BlockSpec(memory_space=pltpu.SMEM)


def here(x):
    return pltpu.with_memory_space_constraint(x, pltpu.VMEM)


def there(x):
    return pltpu.with_memory_space_constraint(x, pltpu.HBM)


def call(kernel, name, arrays, in_specs, out_shape, out_specs, limit, scratch=(), flops=0, moved=0):
    return pl.pallas_call(
        kernel,
        in_specs=in_specs,
        out_specs=out_specs,
        out_shape=out_shape,
        scratch_shapes=list(scratch),
        compiler_params=pltpu.CompilerParams(vmem_limit_bytes=limit * MIB),
        cost_estimate=pl.CostEstimate(flops=int(flops), bytes_accessed=int(moved), transcendentals=0),
        name=name,
    )(*arrays)


def row_copy(source, target, sems, step, i):
    rows = pl.ds(pl.multiple_of(i * step, step), step)
    return pltpu.make_async_copy(source.at[rows], target.at[rows], sems.at[i])


def start_rows(source, target, sems, step):
    for i in range(source.shape[0] // step):
        row_copy(source, target, sems, step, i).start()


def for_rows(source, target, sems, step, work):
    def body(i, carry):
        row_copy(source, target, sems, step, i).wait()
        work(i)
        return carry

    lax.fori_loop(0, source.shape[0] // step, body, 0)


def turned_fold(x):
    return fold3(x.T[:3 * RANK])


def three_terms(q_t):
    terms = [term.astype(F32) for term in split3(q_t)]
    return jnp.concatenate(terms + [jnp.zeros_like(terms[0])], axis=0).T.astype(BF16)


def token_product_kernel(core_ref, q_hbm, g_hbm, x_hbm, t_ref, top_ref, bottom_ref, q_ref, q3_ref, g_ref, sems, g_sems):
    step = 512
    part = t_ref.shape[2]
    half = top_ref.shape[0]
    q_copy = pltpu.make_async_copy(q_hbm, q_ref, sems.at[0])
    halves = [
        pltpu.make_async_copy(x_hbm.at[pl.ds(0, half)], top_ref, sems.at[1]),
        pltpu.make_async_copy(x_hbm.at[pl.ds(half, half)], bottom_ref, sems.at[2]),
    ]
    q_copy.start()
    start_rows(g_hbm, g_ref, g_sems, step)

    @pl.when(core_ref[0] >= 0)
    def _():
        q_copy.wait()
        q3_ref[...] = three_terms(q_ref[...])

    def work(i):
        @pl.when(i == 0)
        def _():
            for copy in halves:
                copy.start()

        for k in range(step // part):
            rows = pl.ds(pl.multiple_of(i * step + k * part, part), part)
            t_ref[i * (step // part) + k] = turned_fold(dot(g_ref[rows, :], q3_ref[...], NN))

    for_rows(g_hbm, g_ref, g_sems, step, work)
    for copy in halves:
        copy.wait()


def token_product(core, q_t, grads, inputs, parts):
    tokens, cols = grads.shape
    half = inputs.shape[0] // 2
    return call(
        token_product_kernel, "token_product", (core, there(q_t), there(grads), there(inputs)), [SMEM_SPEC] + [HBM_SPEC] * 3,
        [
            pltpu.VMEM((parts, RANK, tokens // parts), F32),
            pltpu.VMEM((half, inputs.shape[1]), BF16),
            pltpu.VMEM((half, inputs.shape[1]), BF16),
        ],
        [VMEM_SPEC] * 3, 16,
        [
            pltpu.VMEM(q_t.shape, F32),
            pltpu.VMEM((cols, 4 * RANK), BF16),
            pltpu.VMEM((tokens, cols), BF16),
            pltpu.SemaphoreType.DMA((3,)),
            pltpu.SemaphoreType.DMA((tokens // 512,)),
        ],
        2 * 256 * tokens * cols, 2 * tokens * cols,
    )


def error_product_kernel(core_ref, q_hbm, e_hbm, p_ref, q_ref, q3_ref, e_ref, sem, sems):
    step = 768
    q_copy = pltpu.make_async_copy(q_hbm, q_ref, sem)
    q_copy.start()
    start_rows(e_hbm, e_ref, sems, step)

    @pl.when(core_ref[0] >= 0)
    def _():
        q_copy.wait()
        q3_ref[...] = three_terms(q_ref[...])

    def work(i):
        rows = pl.ds(pl.multiple_of(i * step, step), step)
        p_ref[:, rows] = turned_fold(dot(e_ref[rows, :], q3_ref[...], NN))

    for_rows(e_hbm, e_ref, sems, step, work)


def error_product(core, q_t, error):
    rows, cols = error.shape
    return call(
        error_product_kernel, "error_product", (core, there(q_t), there(error)), [SMEM_SPEC] + [HBM_SPEC] * 2,
        pltpu.VMEM((RANK, rows), F32), VMEM_SPEC, 16,
        [
            pltpu.VMEM(q_t.shape, F32),
            pltpu.VMEM((cols, 4 * RANK), BF16),
            pltpu.VMEM((rows, cols), BF16),
            pltpu.SemaphoreType.DMA,
            pltpu.SemaphoreType.DMA((rows // 768,)),
        ],
        10e9, 0,
    )


def cut_halves(core, full_ref, keep_ref, send_ref):
    half = RANK // 2
    wide = full_ref.shape[1] // 128
    for ref, who in ((keep_ref, core), (send_ref, 1 - core)):
        rows = full_ref[pl.ds(pl.multiple_of(who * half, half), half), :]
        for r in range(half // 8):
            for k in range(wide):
                ref[r * wide + k] = rows[8 * r:8 * r + 8, 128 * k:128 * k + 128]


def join_halves(core, mine_ref, other_ref, full_ref):
    half = RANK // 2
    wide = full_ref.shape[1] // 128
    for ref, who in ((mine_ref, core), (other_ref, 1 - core)):
        for r in range(half // 8):
            rows = pl.ds(pl.multiple_of(who * half + 8 * r, 8), 8)
            for k in range(wide):
                full_ref[rows, 128 * k:128 * k + 128] = ref[r * wide + k]


def left_kernel(core_ref, t_ref, x_ref, e_ref, keep_ref, send_ref, full_ref):
    tokens = (t_ref[0] + t_ref[1]) + (t_ref[2] + t_ref[3])
    full_ref[...] = fold3(dot(stack3(tokens), x_ref[...], NN)) + e_ref[...]
    cut_halves(core_ref[0], full_ref, keep_ref, send_ref)


def left_partial(core, tokens, inputs, error_part):
    rows = inputs.shape[1]
    half = pltpu.VMEM((RANK // 16 * rows // 128, 8, 128), F32)
    return call(
        left_kernel, "left_partial", (core, tokens, inputs, here(error_part)), [SMEM_SPEC] + [VMEM_SPEC] * 3,
        [half, half], [VMEM_SPEC] * 2, 12, [pltpu.VMEM((RANK, rows), F32)],
        2 * 256 * inputs.size, 2 * inputs.size,
    )


def right_kernel(core_ref, mine_ref, other_ref, xt_ref, g_ref, e_ref, keep_ref, send_ref, p_ref, p3_ref, xp_ref, full_ref):
    join_halves(core_ref[0], mine_ref, other_ref, p_ref)
    p3_ref[...] = stack3(p_ref[...])
    xp_ref[...] = stack3(fold3(dot(p3_ref[...], xt_ref[...], NN)))
    step = 256
    for i in range(g_ref.shape[1] // step):
        cols = slice(i * step, (i + 1) * step)
        full_ref[:, cols] = fold3(dot(p3_ref[...], e_ref[:, cols], NN) + dot(xp_ref[...], g_ref[:, cols], NN))
    cut_halves(core_ref[0], full_ref, keep_ref, send_ref)


def right_partial(core, mine, other, inputs_t, grads, error):
    rows, cols = error.shape
    tokens = grads.shape[0]
    half = pltpu.VMEM((RANK // 16 * cols // 128, 8, 128), F32)
    return call(
        right_kernel, "right_partial", (core, mine, other, here(inputs_t), here(grads), here(error)),
        [SMEM_SPEC] + [VMEM_SPEC] * 5,
        [half, half, pltpu.VMEM((RANK, rows), F32)], [VMEM_SPEC] * 3, 12,
        [
            pltpu.VMEM((3 * RANK, rows), BF16),
            pltpu.VMEM((3 * RANK, tokens), BF16),
            pltpu.VMEM((RANK, cols), F32),
        ],
        2 * 256 * (rows * cols + tokens * (rows + cols)), 0,
    )


def turn_kernel(places, at_ref, *refs):
    out_ref = refs[-1]
    tokens = out_ref.shape[1] // 4
    for (by, half), ref in zip(places, refs):
        owner = lax.rem(at_ref[0] + by, 4)
        start = pl.multiple_of(owner * tokens + half * (tokens // 2), 128)
        out_ref[:, pl.ds(start, ref.shape[0])] = ref[...].T


def turned(places, at, pieces, earlier=None, flops=0):
    rows = pieces[0].shape[1]
    arrays = tuple(pieces) if earlier is None else (*pieces, here(earlier))
    return pl.pallas_call(
        functools.partial(turn_kernel, places),
        in_specs=[SMEM_SPEC] + [VMEM_SPEC] * len(arrays),
        out_specs=VMEM_SPEC,
        out_shape=pltpu.VMEM((rows, 8 * pieces[-1].shape[0]), BF16),
        input_output_aliases={} if earlier is None else {len(arrays): 0},
        compiler_params=pltpu.CompilerParams(vmem_limit_bytes=12 * MIB),
        cost_estimate=pl.CostEstimate(flops=int(flops), bytes_accessed=0, transcendentals=0),
        name="turned",
    )(at, *arrays)


def load_kernel(source, target, sem):
    copy = pltpu.make_async_copy(source, target, sem)
    copy.start()
    copy.wait()


def loaded(x, cost):
    return call(
        load_kernel, "loaded", (there(x),), [HBM_SPEC], pltpu.VMEM(x.shape, x.dtype), VMEM_SPEC, 12,
        [pltpu.SemaphoreType.DMA], cost, 0,
    )


def combined_kernel(at, rows, xt_ref, g_ref, e_ref, c_ref):
    here_rows = slice(at * rows, (at + 1) * rows)
    step = 256
    for i in range(g_ref.shape[1] // step):
        cols = slice(i * step, (i + 1) * step)
        c_ref[:, cols] = dot(xt_ref[here_rows, :], g_ref[:, cols], NN) + e_ref[here_rows, cols].astype(F32)


def combined(at, parts, inputs_t, grads, error):
    rows, cols = error.shape
    rows //= parts
    return call(
        functools.partial(combined_kernel, at, rows), "combined", (here(inputs_t), here(grads), here(error)),
        [VMEM_SPEC] * 3, pltpu.VMEM((rows, cols), F32), VMEM_SPEC, 12, (),
        2 * rows * cols * grads.shape[0], 0,
    )


def factor_kernel(p_ref, basis_ref, u6_ref, inv_ref):
    p = p_ref[...]
    gram = lax.dot_general(p, p, NT, precision=lax.Precision.HIGHEST, preferred_element_type=F32)
    row = lax.broadcasted_iota(jnp.int32, (RANK, 1), 0)
    eye = (row == lax.broadcasted_iota(jnp.int32, (RANK, RANK), 1)).astype(F32)
    both = jnp.concatenate([gram, eye], axis=1)
    scale = jnp.zeros((RANK, 1), F32)
    for k in range(RANK):
        pivot = both[k:k + 1, k:k + 1]
        scale = jnp.where(row == k, lax.rsqrt(pivot), scale)
        factor = jnp.where(row > k, both[:, k:k + 1] / pivot, 0.0)
        both = both - factor * both[k:k + 1, :]
    inverse = both[:, RANK:] * scale
    i1, i2, i3 = (term.astype(F32) for term in split3(inverse))
    inv_ref[...] = jnp.concatenate([i1, i1, i1, i2, i2, i3], axis=1).astype(BF16)
    u = lax.dot_general(inverse, p, NN, precision=lax.Precision.HIGHEST, preferred_element_type=F32)
    u1, u2, u3 = (term.astype(F32) for term in split3(u))
    u6 = jnp.concatenate([u1, u2, u3, u1, u2, u1, u, jnp.zeros_like(u)], axis=0).T
    basis_ref[...] = u
    u6_ref[...] = u6[:, :6 * RANK].astype(BF16)


def factor(p):
    rows = p.shape[1]
    return call(
        factor_kernel, "factor", (here(p),), [VMEM_SPEC],
        [pltpu.VMEM((RANK, rows), F32), pltpu.VMEM((rows, 6 * RANK), BF16), pltpu.VMEM((RANK, 6 * RANK), BF16)],
        [VMEM_SPEC] * 3, 12, (), 4e9, 0,
    )


def residual_kernel(replicas, core_ref, mine_ref, other_ref, inv_ref, u_ref, *refs):
    *c_refs, out_hbm, q_ref, full_ref, w6_ref, block_ref, sems = refs
    join_halves(core_ref[0], mine_ref, other_ref, full_ref)
    q1, q2, q3 = split3(full_ref[...])
    w = dot(inv_ref[...], jnp.concatenate([q1, q2, q3, q1, q2, q1], axis=0), NN) * (1.0 / replicas)
    q_ref[...] = w
    w1, w2, w3 = split3(-w)
    w6_ref[...] = jnp.concatenate([w1, w1, w1, w2, w2, w3], axis=0)
    slots, step, width = block_ref.shape
    each = c_refs[0].shape[0] // step

    def copy_out(i):
        rows = pl.ds(pl.multiple_of(i * step, step), step)
        slot = lax.rem(i, slots)
        return pltpu.make_async_copy(block_ref.at[slot], out_hbm.at[0, rows], sems.at[slot])

    def part(s, c_ref):
        def body(k, carry):
            i = s * each + k
            slot = lax.rem(i, slots)
            rows = pl.ds(pl.multiple_of(i * step, step), step)
            c_rows = pl.ds(pl.multiple_of(k * step, step), step)

            @pl.when(i >= slots)
            def _():
                copy_out(i - slots).wait()

            for at in range(0, width, 256):
                cols = slice(at, at + 256)
                update = dot(u_ref[rows, :], w6_ref[:, cols], NN)
                block_ref[slot, :, cols] = (c_ref[c_rows, cols] + update).astype(BF16)
            copy_out(i).start()
            return carry

        lax.fori_loop(0, each, body, 0)

    for s, c_ref in enumerate(c_refs):
        part(s, c_ref)
    count = each * len(c_refs)
    for i in range(count - slots, count):
        copy_out(i).wait()


def residual(core, mine, other, inverse, u6, parts, replicas):
    cols = parts[0].shape[1]
    rows = len(parts) * parts[0].shape[0]
    step = parts[0].shape[0] // 2
    return call(
        functools.partial(residual_kernel, replicas), "residual",
        (core, mine, other, here(inverse), here(u6), *(here(part) for part in parts)),
        [SMEM_SPEC] + [VMEM_SPEC] * (4 + len(parts)),
        [pltpu.HBM((1, rows, cols), BF16), jax.ShapeDtypeStruct((RANK, cols), F32)],
        [HBM_SPEC, VMEM_SPEC], 12,
        [
            pltpu.VMEM((RANK, cols), F32),
            pltpu.VMEM((6 * RANK, cols), BF16),
            pltpu.VMEM((3, step, cols), BF16),
            pltpu.SemaphoreType.DMA((3,)),
        ],
        2 * 256 * rows * cols, 2 * rows * cols,
    )


def swap(x, axis, pairs):
    return lax.ppermute(x, axis, [(a, b) for a, b in pairs] + [(b, a) for a, b in pairs])


def shift(x, by):
    return lax.ppermute(x, "z", [(i, (i + by) % 4) for i in range(4)])


FIRST, SECOND = [(0, 1), (2, 3)], [(1, 2), (3, 0)]


def after(reason, *arrays):
    return lax.optimization_barrier((reason, *arrays))[1:]


def add_swapped(x, axis, pairs, *with_it):
    moved = swap(x, axis, pairs)
    return x + lax.optimization_barrier((moved, *with_it))[0]


def local(layer_input, output_grad, error_buffer, q_start):
    inputs, grads, error = layer_input[0], output_grad[0], error_buffer[0]
    core = lax.axis_index("c").astype(jnp.int32)[None]
    at = lax.axis_index("z").astype(jnp.int32)[None]
    replicas = 32
    tokens, top, bottom = token_product(core, q_start.T, grads, inputs, 4)
    (q_t,) = after(tokens, q_start.T)
    tokens = lax.all_to_all(tokens, "z", 0, 0)
    left_a, right_b = shift(top, 1), shift(bottom, -1)
    error_part = error_product(core, q_t, error)
    keep, send = left_partial(core, tokens, inputs, error_part)
    p = keep + swap(send, "c", [(0, 1)])
    p = add_swapped(p, "z", FIRST)
    bottom, top = after(p, bottom, top)
    left_b, right_a = shift(bottom, 1), shift(top, -1)
    inputs_t = turned(((0, 0), (3, 0), (1, 1)), at, after(p, inputs, left_a, right_b), None, 4e9)
    p = add_swapped(p, "z", SECOND, inputs_t)
    far_a, far_b = after(p, left_a, right_b)
    far_a, far_b = shift(far_a, 1), shift(far_b, -1)
    p = add_swapped(p, "x", FIRST)
    error = loaded(*after(p, error), 4e9)
    p = add_swapped(p, "x", SECOND, error)
    left_b, right_a, inputs_t, grads = after(p, left_b, right_a, inputs_t, grads)
    grads = loaded(grads, 2e9)
    inputs_t = turned(((3, 1), (1, 0)), at, (left_b, right_a), inputs_t, 2e9)
    p = add_swapped(p, "y", FIRST, grads, inputs_t)
    far_a, far_b, inputs_t = after(p, far_a, far_b, inputs_t)
    inputs_t = turned(((2, 0), (2, 1)), at, (far_a, far_b), inputs_t, 0)
    p = add_swapped(p, "y", SECOND, inputs_t)
    keep, send, p = right_partial(core, p, swap(p, "c", [(0, 1)]), inputs_t, grads, error)

    q = keep + swap(send, "c", [(0, 1)])
    basis, u6, inverse = factor(*after(q, p))
    q = add_swapped(q, "x", FIRST, basis)
    parts = []
    for s, (axis, pairs) in enumerate((("x", SECOND), ("y", FIRST), ("y", SECOND))):
        parts.append(combined(s, 3, *after(q, inputs_t, grads, error)))
        q = add_swapped(q, axis, pairs, parts[-1])
    other = swap(q, "c", [(0, 1)])
    error_next, q_next = residual(core, q, other, inverse, u6, parts, replicas)
    return error_next, basis.T, q_next.T


def solution(mesh):
    fine = Mesh(mesh.devices.reshape(4, 4, 2, 4), ("x", "y", "c", "z"))
    dp = ("x", "y", "c")
    in_specs = (P(dp, "z", None), P(dp, None, "z"), P(dp, None, "z"), P("z", None))
    out_specs = (P(dp, None, "z"), P(), P("z", None))
    return jax.shard_map(local, mesh=fine, in_specs=in_specs, out_specs=out_specs, check_vma=False)
```

```python
import functools

import jax
import jax.numpy as jnp
from jax import lax
from jax.experimental import pallas as pl
from jax.experimental.pallas import tpu as pltpu
from jax.sharding import Mesh, PartitionSpec as P

F32, BF16 = jnp.float32, jnp.bfloat16
MIB = 1 << 20
RANK = 32
NN = (((1,), (0,)), ((), ()))
NT = (((1,), (1,)), ((), ()))


def split3(x):
    hi = x.astype(BF16)
    rest = x - hi.astype(F32)
    mid = rest.astype(BF16)
    low = (rest - mid.astype(F32)).astype(BF16)
    return hi, mid, low


def stack3(x):
    return jnp.concatenate(split3(x), axis=0)


def fold3(x):
    return (x[2 * RANK:] + x[RANK:2 * RANK]) + x[:RANK]


def dot(a, b, dims):
    return lax.dot_general(a, b, dims, preferred_element_type=F32)


VMEM_SPEC = pl.BlockSpec(memory_space=pltpu.VMEM)
HBM_SPEC = pl.BlockSpec(memory_space=pltpu.HBM)
SMEM_SPEC = pl.BlockSpec(memory_space=pltpu.SMEM)


def here(x):
    return pltpu.with_memory_space_constraint(x, pltpu.VMEM)


def there(x):
    return pltpu.with_memory_space_constraint(x, pltpu.HBM)


def call(kernel, name, arrays, in_specs, out_shape, out_specs, limit, scratch=(), flops=0, moved=0):
    return pl.pallas_call(
        kernel,
        in_specs=in_specs,
        out_specs=out_specs,
        out_shape=out_shape,
        scratch_shapes=list(scratch),
        compiler_params=pltpu.CompilerParams(vmem_limit_bytes=limit * MIB),
        cost_estimate=pl.CostEstimate(flops=int(flops), bytes_accessed=int(moved), transcendentals=0),
        name=name,
    )(*arrays)


def row_copy(source, target, sems, step, i):
    rows = pl.ds(pl.multiple_of(i * step, step), step)
    return pltpu.make_async_copy(source.at[rows], target.at[rows], sems.at[i])


def start_rows(source, target, sems, step):
    for i in range(source.shape[0] // step):
        row_copy(source, target, sems, step, i).start()


def for_rows(source, target, sems, step, work):
    def body(i, carry):
        row_copy(source, target, sems, step, i).wait()
        work(i)
        return carry

    lax.fori_loop(0, source.shape[0] // step, body, 0)


def turned_fold(x):
    return fold3(x.T[:3 * RANK])


def three_terms(q_t):
    terms = [term.astype(F32) for term in split3(q_t)]
    return jnp.concatenate(terms + [jnp.zeros_like(terms[0])], axis=0).T.astype(BF16)


def token_product_kernel(core_ref, q_hbm, g_hbm, x_hbm, t_ref, top_ref, bottom_ref, q_ref, q3_ref, g_ref, sems, g_sems):
    step = 512
    part = t_ref.shape[2]
    half = top_ref.shape[0]
    q_copy = pltpu.make_async_copy(q_hbm, q_ref, sems.at[0])
    halves = [
        pltpu.make_async_copy(x_hbm.at[pl.ds(0, half)], top_ref, sems.at[1]),
        pltpu.make_async_copy(x_hbm.at[pl.ds(half, half)], bottom_ref, sems.at[2]),
    ]
    q_copy.start()
    start_rows(g_hbm, g_ref, g_sems, step)
    for copy in halves:
        copy.start()

    @pl.when(core_ref[0] >= 0)
    def _():
        q_copy.wait()
        q3_ref[...] = three_terms(q_ref[...])

    def work(i):
        for k in range(step // part):
            rows = pl.ds(pl.multiple_of(i * step + k * part, part), part)
            t_ref[i * (step // part) + k] = turned_fold(dot(g_ref[rows, :], q3_ref[...], NN))

    for_rows(g_hbm, g_ref, g_sems, step, work)
    for copy in halves:
        copy.wait()


def token_product(core, q_t, grads, inputs, parts):
    tokens, cols = grads.shape
    half = inputs.shape[0] // 2
    return call(
        token_product_kernel, "token_product", (core, there(q_t), there(grads), there(inputs)), [SMEM_SPEC] + [HBM_SPEC] * 3,
        [
            pltpu.VMEM((parts, RANK, tokens // parts), F32),
            pltpu.VMEM((half, inputs.shape[1]), BF16),
            pltpu.VMEM((half, inputs.shape[1]), BF16),
        ],
        [VMEM_SPEC] * 3, 16,
        [
            pltpu.VMEM(q_t.shape, F32),
            pltpu.VMEM((cols, 4 * RANK), BF16),
            pltpu.VMEM((tokens, cols), BF16),
            pltpu.SemaphoreType.DMA((3,)),
            pltpu.SemaphoreType.DMA((tokens // 512,)),
        ],
        2 * 256 * tokens * cols, 2 * tokens * cols,
    )


def error_product_kernel(core_ref, q_hbm, e_hbm, p_ref, q_ref, q3_ref, e_ref, sem, sems):
    step = 768
    q_copy = pltpu.make_async_copy(q_hbm, q_ref, sem)
    q_copy.start()
    start_rows(e_hbm, e_ref, sems, step)

    @pl.when(core_ref[0] >= 0)
    def _():
        q_copy.wait()
        q3_ref[...] = three_terms(q_ref[...])

    def work(i):
        rows = pl.ds(pl.multiple_of(i * step, step), step)
        p_ref[:, rows] = turned_fold(dot(e_ref[rows, :], q3_ref[...], NN))

    for_rows(e_hbm, e_ref, sems, step, work)


def error_product(core, q_t, error):
    rows, cols = error.shape
    return call(
        error_product_kernel, "error_product", (core, there(q_t), there(error)), [SMEM_SPEC] + [HBM_SPEC] * 2,
        pltpu.VMEM((RANK, rows), F32), VMEM_SPEC, 16,
        [
            pltpu.VMEM(q_t.shape, F32),
            pltpu.VMEM((cols, 4 * RANK), BF16),
            pltpu.VMEM((rows, cols), BF16),
            pltpu.SemaphoreType.DMA,
            pltpu.SemaphoreType.DMA((rows // 768,)),
        ],
        10e9, 0,
    )


def cut_halves(core, full_ref, keep_ref, send_ref):
    half = RANK // 2
    wide = full_ref.shape[1] // 128
    for ref, who in ((keep_ref, core), (send_ref, 1 - core)):
        rows = full_ref[pl.ds(pl.multiple_of(who * half, half), half), :]
        for r in range(half // 8):
            for k in range(wide):
                ref[r * wide + k] = rows[8 * r:8 * r + 8, 128 * k:128 * k + 128]


def join_halves(core, mine_ref, other_ref, full_ref):
    half = RANK // 2
    wide = full_ref.shape[1] // 128
    for ref, who in ((mine_ref, core), (other_ref, 1 - core)):
        for r in range(half // 8):
            rows = pl.ds(pl.multiple_of(who * half + 8 * r, 8), 8)
            for k in range(wide):
                full_ref[rows, 128 * k:128 * k + 128] = ref[r * wide + k]


def left_kernel(core_ref, t_ref, x_ref, e_ref, keep_ref, send_ref, full_ref):
    tokens = (t_ref[0] + t_ref[1]) + (t_ref[2] + t_ref[3])
    full_ref[...] = fold3(dot(stack3(tokens), x_ref[...], NN)) + e_ref[...]
    cut_halves(core_ref[0], full_ref, keep_ref, send_ref)


def left_partial(core, tokens, inputs, error_part):
    rows = inputs.shape[1]
    half = pltpu.VMEM((RANK // 16 * rows // 128, 8, 128), F32)
    return call(
        left_kernel, "left_partial", (core, tokens, inputs, here(error_part)), [SMEM_SPEC] + [VMEM_SPEC] * 3,
        [half, half], [VMEM_SPEC] * 2, 12, [pltpu.VMEM((RANK, rows), F32)],
        2 * 256 * inputs.size, 2 * inputs.size,
    )


def right_kernel(core_ref, mine_ref, other_ref, xt_ref, g_ref, e_ref, keep_ref, send_ref, p_ref, p3_ref, xp_ref, full_ref):
    join_halves(core_ref[0], mine_ref, other_ref, p_ref)
    p3_ref[...] = stack3(p_ref[...])
    xp_ref[...] = stack3(fold3(dot(p3_ref[...], xt_ref[...], NN)))
    step = 256
    for i in range(g_ref.shape[1] // step):
        cols = slice(i * step, (i + 1) * step)
        full_ref[:, cols] = fold3(dot(p3_ref[...], e_ref[:, cols], NN) + dot(xp_ref[...], g_ref[:, cols], NN))
    cut_halves(core_ref[0], full_ref, keep_ref, send_ref)


def right_partial(core, mine, other, inputs_t, grads, error):
    rows, cols = error.shape
    tokens = grads.shape[0]
    half = pltpu.VMEM((RANK // 16 * cols // 128, 8, 128), F32)
    return call(
        right_kernel, "right_partial", (core, mine, other, here(inputs_t), here(grads), here(error)),
        [SMEM_SPEC] + [VMEM_SPEC] * 5,
        [half, half, pltpu.VMEM((RANK, rows), F32)], [VMEM_SPEC] * 3, 12,
        [
            pltpu.VMEM((3 * RANK, rows), BF16),
            pltpu.VMEM((3 * RANK, tokens), BF16),
            pltpu.VMEM((RANK, cols), F32),
        ],
        2 * 256 * (rows * cols + tokens * (rows + cols)), 0,
    )


def turn_kernel(places, at_ref, *refs):
    out_ref = refs[-1]
    tokens = out_ref.shape[1] // 4
    for (by, half), ref in zip(places, refs):
        owner = lax.rem(at_ref[0] + by, 4)
        start = pl.multiple_of(owner * tokens + half * (tokens // 2), 128)
        out_ref[:, pl.ds(start, ref.shape[0])] = ref[...].T


def turned(places, at, pieces, earlier=None, flops=0):
    rows = pieces[0].shape[1]
    arrays = tuple(pieces) if earlier is None else (*pieces, here(earlier))
    return pl.pallas_call(
        functools.partial(turn_kernel, places),
        in_specs=[SMEM_SPEC] + [VMEM_SPEC] * len(arrays),
        out_specs=VMEM_SPEC,
        out_shape=pltpu.VMEM((rows, 8 * pieces[-1].shape[0]), BF16),
        input_output_aliases={} if earlier is None else {len(arrays): 0},
        compiler_params=pltpu.CompilerParams(vmem_limit_bytes=12 * MIB),
        cost_estimate=pl.CostEstimate(flops=int(flops), bytes_accessed=0, transcendentals=0),
        name="turned",
    )(at, *arrays)


def load_kernel(source, target, sem):
    copy = pltpu.make_async_copy(source, target, sem)
    copy.start()
    copy.wait()


def loaded(x, cost):
    return call(
        load_kernel, "loaded", (there(x),), [HBM_SPEC], pltpu.VMEM(x.shape, x.dtype), VMEM_SPEC, 12,
        [pltpu.SemaphoreType.DMA], cost, 0,
    )


def combined_kernel(at, rows, xt_ref, g_ref, e_ref, c_ref):
    here_rows = slice(at * rows, (at + 1) * rows)
    step = 256
    for i in range(g_ref.shape[1] // step):
        cols = slice(i * step, (i + 1) * step)
        c_ref[:, cols] = dot(xt_ref[here_rows, :], g_ref[:, cols], NN) + e_ref[here_rows, cols].astype(F32)


def combined(at, parts, inputs_t, grads, error):
    rows, cols = error.shape
    rows //= parts
    return call(
        functools.partial(combined_kernel, at, rows), "combined", (here(inputs_t), here(grads), here(error)),
        [VMEM_SPEC] * 3, pltpu.VMEM((rows, cols), F32), VMEM_SPEC, 12, (),
        2 * rows * cols * grads.shape[0], 0,
    )


def factor_kernel(p_ref, basis_ref, u6_ref, inv_ref):
    p = p_ref[...]
    gram = lax.dot_general(p, p, NT, precision=lax.Precision.HIGHEST, preferred_element_type=F32)
    row = lax.broadcasted_iota(jnp.int32, (RANK, 1), 0)
    eye = (row == lax.broadcasted_iota(jnp.int32, (RANK, RANK), 1)).astype(F32)
    both = jnp.concatenate([gram, eye], axis=1)
    scale = jnp.zeros((RANK, 1), F32)
    for k in range(RANK):
        pivot = both[k:k + 1, k:k + 1]
        scale = jnp.where(row == k, lax.rsqrt(pivot), scale)
        factor = jnp.where(row > k, both[:, k:k + 1] / pivot, 0.0)
        both = both - factor * both[k:k + 1, :]
    inverse = both[:, RANK:] * scale
    i1, i2, i3 = (term.astype(F32) for term in split3(inverse))
    inv_ref[...] = jnp.concatenate([i1, i1, i1, i2, i2, i3], axis=1).astype(BF16)
    u = lax.dot_general(inverse, p, NN, precision=lax.Precision.HIGHEST, preferred_element_type=F32)
    u1, u2, u3 = (term.astype(F32) for term in split3(u))
    u6 = jnp.concatenate([u1, u2, u3, u1, u2, u1, u, jnp.zeros_like(u)], axis=0).T
    basis_ref[...] = u
    u6_ref[...] = u6[:, :6 * RANK].astype(BF16)


def factor(p):
    rows = p.shape[1]
    return call(
        factor_kernel, "factor", (here(p),), [VMEM_SPEC],
        [pltpu.VMEM((RANK, rows), F32), pltpu.VMEM((rows, 6 * RANK), BF16), pltpu.VMEM((RANK, 6 * RANK), BF16)],
        [VMEM_SPEC] * 3, 12, (), 4e9, 0,
    )


def residual_kernel(replicas, core_ref, mine_ref, other_ref, inv_ref, u_ref, *refs):
    *c_refs, out_hbm, q_ref, full_ref, w6_ref, block_ref, sems = refs
    join_halves(core_ref[0], mine_ref, other_ref, full_ref)
    q1, q2, q3 = split3(full_ref[...])
    w = dot(inv_ref[...], jnp.concatenate([q1, q2, q3, q1, q2, q1], axis=0), NN) * (1.0 / replicas)
    q_ref[...] = w
    w1, w2, w3 = split3(-w)
    w6_ref[...] = jnp.concatenate([w1, w1, w1, w2, w2, w3], axis=0)
    slots, step, width = block_ref.shape
    each = c_refs[0].shape[0] // step

    def copy_out(i):
        rows = pl.ds(pl.multiple_of(i * step, step), step)
        slot = lax.rem(i, slots)
        return pltpu.make_async_copy(block_ref.at[slot], out_hbm.at[0, rows], sems.at[slot])

    def part(s, c_ref):
        def body(k, carry):
            i = s * each + k
            slot = lax.rem(i, slots)
            rows = pl.ds(pl.multiple_of(i * step, step), step)
            c_rows = pl.ds(pl.multiple_of(k * step, step), step)

            @pl.when(i >= slots)
            def _():
                copy_out(i - slots).wait()

            for at in range(0, width, 256):
                cols = slice(at, at + 256)
                update = dot(u_ref[rows, :], w6_ref[:, cols], NN)
                block_ref[slot, :, cols] = (c_ref[c_rows, cols] + update).astype(BF16)
            copy_out(i).start()
            return carry

        lax.fori_loop(0, each, body, 0)

    for s, c_ref in enumerate(c_refs):
        part(s, c_ref)
    count = each * len(c_refs)
    for i in range(count - slots, count):
        copy_out(i).wait()


def residual(core, mine, other, inverse, u6, parts, replicas):
    cols = parts[0].shape[1]
    rows = len(parts) * parts[0].shape[0]
    step = parts[0].shape[0] // 2
    return call(
        functools.partial(residual_kernel, replicas), "residual",
        (core, mine, other, here(inverse), here(u6), *(here(part) for part in parts)),
        [SMEM_SPEC] + [VMEM_SPEC] * (4 + len(parts)),
        [pltpu.HBM((1, rows, cols), BF16), jax.ShapeDtypeStruct((RANK, cols), F32)],
        [HBM_SPEC, VMEM_SPEC], 12,
        [
            pltpu.VMEM((RANK, cols), F32),
            pltpu.VMEM((6 * RANK, cols), BF16),
            pltpu.VMEM((3, step, cols), BF16),
            pltpu.SemaphoreType.DMA((3,)),
        ],
        2 * 256 * rows * cols, 2 * rows * cols,
    )


def swap(x, axis, pairs):
    return lax.ppermute(x, axis, [(a, b) for a, b in pairs] + [(b, a) for a, b in pairs])


def shift(x, by):
    return lax.ppermute(x, "z", [(i, (i + by) % 4) for i in range(4)])


FIRST, SECOND = [(0, 1), (2, 3)], [(1, 2), (3, 0)]


def after(reason, *arrays):
    return lax.optimization_barrier((reason, *arrays))[1:]


def add_swapped(x, axis, pairs, *with_it):
    moved = swap(x, axis, pairs)
    return x + lax.optimization_barrier((moved, *with_it))[0]


def local(layer_input, output_grad, error_buffer, q_start):
    inputs, grads, error = layer_input[0], output_grad[0], error_buffer[0]
    core = lax.axis_index("c").astype(jnp.int32)[None]
    at = lax.axis_index("z").astype(jnp.int32)[None]
    replicas = 32
    tokens, top, bottom = token_product(core, q_start.T, grads, inputs, 4)
    (q_t,) = after(tokens, q_start.T)
    tokens = lax.all_to_all(tokens, "z", 0, 0)
    left_a, right_b = shift(top, 1), shift(bottom, -1)
    error_part = error_product(core, q_t, error)
    keep, send = left_partial(core, tokens, inputs, error_part)
    p = keep + swap(send, "c", [(0, 1)])
    error = loaded(*after(p, error), 4e9)
    p = add_swapped(p, "z", FIRST, error)
    bottom, top = after(p, bottom, top)
    left_b, right_a = shift(bottom, 1), shift(top, -1)
    inputs_t = turned(((0, 0), (3, 0), (1, 1)), at, after(p, inputs, left_a, right_b), None, 4e9)
    p = add_swapped(p, "z", SECOND, inputs_t)
    far_a, far_b = after(p, left_a, right_b)
    far_a, far_b = shift(far_a, 1), shift(far_b, -1)
    p = add_swapped(p, "x", FIRST)
    p = add_swapped(p, "x", SECOND)
    left_b, right_a, inputs_t, grads = after(p, left_b, right_a, inputs_t, grads)
    grads = loaded(grads, 2e9)
    inputs_t = turned(((3, 1), (1, 0)), at, (left_b, right_a), inputs_t, 2e9)
    p = add_swapped(p, "y", FIRST, grads, inputs_t)
    far_a, far_b, inputs_t = after(p, far_a, far_b, inputs_t)
    inputs_t = turned(((2, 0), (2, 1)), at, (far_a, far_b), inputs_t, 0)
    p = add_swapped(p, "y", SECOND, inputs_t)
    keep, send, p = right_partial(core, p, swap(p, "c", [(0, 1)]), inputs_t, grads, error)

    q = keep + swap(send, "c", [(0, 1)])
    basis, u6, inverse = factor(*after(q, p))
    q = add_swapped(q, "x", FIRST, basis)
    parts = []
    for s, (axis, pairs) in enumerate((("x", SECOND), ("y", FIRST), ("y", SECOND))):
        parts.append(combined(s, 3, *after(q, inputs_t, grads, error)))
        q = add_swapped(q, axis, pairs, parts[-1])
    other = swap(q, "c", [(0, 1)])
    error_next, q_next = residual(core, q, other, inverse, u6, parts, replicas)
    return error_next, basis.T, q_next.T


def solution(mesh):
    fine = Mesh(mesh.devices.reshape(4, 4, 2, 4), ("x", "y", "c", "z"))
    dp = ("x", "y", "c")
    in_specs = (P(dp, "z", None), P(dp, None, "z"), P(dp, None, "z"), P("z", None))
    out_specs = (P(dp, None, "z"), P(), P("z", None))
    return jax.shard_map(local, mesh=fine, in_specs=in_specs, out_specs=out_specs, check_vma=False)
```
